256 devices in a mesh: ta: 8 (over y, z_lo), sa: 32 (over z_hi, x, core).
Axes of the slice: x: 4, y: 4, z: 8 (z_hi: 4, z_lo: 2; z = z_hi * 2 + z_lo), core: 2. Of those that a mesh axis runs over, the one named last changes fastest.
Arguments:
- series: float32 [512, 65536], P('sa', 'ta'), may hold values from -6 to 6
- index_series: float32 [16, 65536], P(None, 'ta'), may hold values from -6 to 6
- assign: int32 [512], replicated, may hold values from 0 to 15
Outputs:
- autocorr: float32 [512, 4096], P('sa', 'ta')
- crosscorr: float32 [512, 4096], P('sa', 'ta')
The draws below stay inside these ranges and needn't reach their ends.
Inputs may be any that keep to these rules, and one draw needn't show every extreme that they name: `assign`: each series names one index series.
All inputs are finite; a program needn't handle non-finite values.
Results may differ from the reference program's by a relative error of at most 0.000098.
Values sent between devices are 32-bit elements; how exact they have to be, the bound alone decides.
No kernel may reach another device: no remote copies, remote signals or barrier semaphores. Data moves between devices by JAX's collectives and lax.ppermute only.
A program may use at most 64 MiB of HBM per device.

```python
import jax
import jax.numpy as jnp

NIDX = 16
TIME = 65536
LAGS = 4096
SERIES = 512


def set_ends(array, rng, smallest, largest):
    spot = [jax.random.randint(jax.random.fold_in(rng, axis), (), 0, length) for axis, length in enumerate(array.shape)]
    widest = array.shape.index(max(array.shape))
    next_to = spot[:widest] + [(spot[widest] + 1) % array.shape[widest]] + spot[widest + 1:]
    return array.at[tuple(spot)].set(smallest).at[tuple(next_to)].set(largest)


def block_scale(own_key, shape, pieces, low, high):
    level = 1.0
    for dim, blocks in pieces:
        steps = jax.random.uniform(jax.random.fold_in(jax.random.fold_in(own_key, 6), dim), (blocks,), jnp.float32, low / len(pieces), high / len(pieces))
        level = level * jnp.repeat(jnp.exp(steps), shape[dim] // blocks).reshape((-1,) + (1,) * (len(shape) - 1 - dim))
    return level


def noise(key, dims, deviation, reach, pieces=(), held_as=jnp.bfloat16):
    loudness = block_scale(key, dims, pieces, -0.22, 0.18) if pieces else 1.0
    values = jax.random.normal(key, dims, jnp.float32) * deviation * loudness
    return jnp.minimum(jnp.maximum(values, -reach), reach).astype(held_as)


def setup_inputs(seed: int = 0) -> dict:
    key_of = jax.random.split(jax.random.key(seed), 4)
    series = noise(key_of[0], (SERIES, TIME), 1.0, 6.0, ((0, 32), (1, 8)), jnp.float32)
    index_series = noise(key_of[1], (NIDX, TIME), 1.0, 6.0, ((1, 8),), jnp.float32)
    assign = set_ends(jax.random.randint(key_of[2], (SERIES,), 0, NIDX), jax.random.fold_in(key_of[2], 1), 0, NIDX - 1).astype(jnp.int32)
    return {"series": series, "index_series": index_series, "assign": assign}


def reference(series, index_series, assign):
    fft_len = 2 * TIME
    spectrum = jnp.fft.rfft(series, n=fft_len, axis=1)
    index_spec = jnp.fft.rfft(index_series, n=fft_len, axis=1)
    partner = index_spec[assign]
    power_spec = spectrum.real * spectrum.real + spectrum.imag * spectrum.imag
    cross_spec = jnp.conj(spectrum) * partner
    factor = 1.0 / jnp.sqrt(jnp.float32(TIME))
    autocorr = jnp.fft.irfft(power_spec, n=fft_len, axis=1)[:, :LAGS] * factor
    crosscorr = jnp.fft.irfft(cross_spec, n=fft_len, axis=1)[:, :LAGS] * factor
    return (autocorr.astype(jnp.float32), crosscorr.astype(jnp.float32))
```

```python
import functools
import math

import jax
import jax.numpy as jnp
import numpy as np
from jax import lax
from jax.experimental import pallas as pl
from jax.experimental.pallas import tpu as pltpu
from jax.sharding import PartitionSpec as P

LANES = 128
ROWS = 32
BLOCK = ROWS * LANES
FFT = 2 * BLOCK
BF16 = jnp.bfloat16
F32 = jnp.float32


def split_np(table):
    hi = table.astype(np.float32).astype(BF16)
    lo = (table - hi.astype(np.float64)).astype(np.float32).astype(BF16)
    return hi, lo


def tables(scale):
    k1 = np.arange(ROWS)[:, None] + 0.5
    t1 = np.arange(ROWS)[None, :]
    first = 2.0 * math.pi * k1 * t1 / (2 * ROWS)
    w1 = np.concatenate([np.cos(first), -np.sin(first)], axis=0)
    w1_hi, w1_lo = split_np(w1)
    w1_cat = np.concatenate([w1_hi, w1_lo, w1_hi], axis=1)
    t2 = np.arange(LANES)[None, :]
    turn = 2.0 * math.pi * k1 * t2 / FFT
    tw = np.stack([np.cos(turn), np.sin(turn)])
    sign = np.where(np.arange(ROWS) % 2 == 0, 1.0, -1.0)[:, None]
    tw_halo = np.stack([np.sin(turn) * sign, -np.cos(turn) * sign])
    second = 2.0 * math.pi * np.arange(LANES)[:, None] * np.arange(LANES)[None, :] / LANES
    c, s = np.cos(second), np.sin(second)
    fwd = np.concatenate([np.concatenate([c, -s], 1), np.concatenate([s, c], 1)], 0)
    inv = np.concatenate([np.concatenate([c, s], 1), np.concatenate([-s, c], 1)], 0)
    n1 = np.arange(ROWS).reshape(8, 4).T.reshape(-1)[:, None]
    last = 2.0 * math.pi * (np.arange(ROWS)[None, :] + 0.5) * n1 / (2 * ROWS)
    w4 = np.concatenate([np.cos(last), -np.sin(last)], axis=1) * scale
    w4_hi, w4_lo = split_np(w4)
    w4_cat = np.concatenate([w4_hi, w4_lo, w4_hi], axis=1)
    return dict(
        w1=w1_cat,
        tw=tw.astype(np.float32),
        tw_halo=tw_halo.astype(np.float32),
        sign=np.broadcast_to(sign, (ROWS, LANES)).astype(np.float32),
        fwd=np.stack(split_np(fwd)),
        inv=np.stack(split_np(inv)),
        w4=w4_cat,
    )


def split(value):
    hi = value.astype(BF16)
    return hi, (value - hi.astype(F32)).astype(BF16)


def dot(a, b):
    return jnp.dot(a, b, preferred_element_type=F32)


def first_stage(blocks, w1, tw_c, tw_s):
    hi, lo = split(jnp.concatenate(blocks, axis=1))
    both = dot(w1, jnp.concatenate([hi, hi, lo], axis=0))
    done = []
    for i in range(2):
        re = both[:ROWS, i * LANES : (i + 1) * LANES]
        im = both[ROWS:, i * LANES : (i + 1) * LANES]
        done.append(jnp.concatenate([re * tw_c + im * tw_s, im * tw_c - re * tw_s], axis=1))
    return done


def second_stage(value, f_hi, f_lo):
    hi, lo = split(value)
    return dot(hi, f_hi) + dot(lo, f_hi) + dot(hi, f_lo)


def parts(value):
    return value[:, :LANES], value[:, LANES:]


def mul_conj(a, b):
    (ar, ai), (br, bi) = a, b
    return ar * br + ai * bi, ai * br - ar * bi


def local_kernel(assign_ref, x_ref, y_ref, w1_ref, tw_ref, sign_ref, f_ref, pre_ref, x0_ref, y0_ref, ys_ref):
    w1 = w1_ref[...]
    tw_c, tw_s = tw_ref[0], tw_ref[1]
    f_hi, f_lo = f_ref[0], f_ref[1]
    sign = sign_ref[...]
    base = lax.axis_index("sa") * 16

    def spectra(ref, series):
        staged = []
        for s in series:
            start = (s // 8) * 512 + s % 8
            blocks = [ref[pl.ds(start + b * 256, ROWS, stride=8), :] for b in range(2)]
            staged += first_stage(blocks, w1, tw_c, tw_s)
        return second_stage(jnp.concatenate(staged, axis=0), f_hi, f_lo)

    group = 4
    for g in range(0, 16, group):
        ys_ref[pl.ds(g * 64, group * 64), :] = spectra(y_ref, range(g, g + group))
    for g in range(0, 16, group):
        spec = spectra(x_ref, range(g, g + group))
        for i in range(group):
            s = g + i
            x0 = spec[i * 64 : i * 64 + ROWS]
            x1 = parts(spec[i * 64 + ROWS : i * 64 + 64])
            x0_ref[s] = x0
            x0 = parts(x0)
            at = pl.multiple_of(assign_ref[base + s] * 64, 64)
            y0 = ys_ref[pl.ds(at, ROWS), :]
            y1 = parts(ys_ref[pl.ds(at + ROWS, ROWS), :])
            y0_ref[s] = y0
            y0 = parts(y0)
            window = (x1[0] - sign * x0[1], x1[1] + sign * x0[0])
            re, im = mul_conj(x1, window)
            pre_ref[s, 0] = jnp.concatenate([re + x0[0] * x0[0] + x0[1] * x0[1], im], axis=1)
            re, im = mul_conj(y1, window)
            re0, im0 = mul_conj(y0, x0)
            pre_ref[s, 1] = jnp.concatenate([re + re0, im + im0], axis=1)


def halo_kernel(h_ref, pre_ref, x0_ref, y0_ref, w1_ref, twh_ref, tw_ref, f_ref, i_ref, w4_ref, out_ref):
    w1 = w1_ref[...]
    tw_c, tw_s = tw_ref[0], tw_ref[1]
    twh_c, twh_s = twh_ref[0], twh_ref[1]
    f_hi, f_lo = f_ref[0], f_ref[1]
    i_hi, i_lo = i_ref[0], i_ref[1]
    w4 = w4_ref[...]
    group = 8
    for g in range(0, 16, group):
        staged = []
        for s in range(g, g + group, 2):
            blocks = [h_ref[pl.ds((q // 8) * 256 + q % 8, ROWS, stride=8), :] for q in (s, s + 1)]
            staged += first_stage(blocks, w1, twh_c, twh_s)
        spec = second_stage(jnp.concatenate(staged, axis=0), f_hi, f_lo)
        whole = []
        for i in range(group):
            s = g + i
            before = parts(spec[i * ROWS : (i + 1) * ROWS])
            for c, other in enumerate((x0_ref, y0_ref)):
                re, im = mul_conj(parts(other[s]), before)
                whole.append(pre_ref[s, c] + jnp.concatenate([re, im], axis=1))
        back = second_stage(jnp.concatenate(whole, axis=0), i_hi, i_lo)
        for i in range(group):
            s = g + i
            turned = []
            for c in range(2):
                re, im = parts(back[(2 * i + c) * ROWS : (2 * i + c + 1) * ROWS])
                turned.append(jnp.concatenate([re * tw_c - im * tw_s, re * tw_s + im * tw_c], axis=0))
            hi, lo = split(jnp.concatenate(turned, axis=1))
            lags = dot(w4, jnp.concatenate([hi, hi, lo], axis=0))
            for c in range(2):
                for low in range(4):
                    out_ref[pl.ds(c * 64 + (s // 8) * 32 + low * 8 + s % 8, 8, stride=128), :] = lags[
                        low * 8 : low * 8 + 8, c * LANES : (c + 1) * LANES
                    ]


VMEM = pl.BlockSpec(memory_space=pltpu.VMEM)
SMEM = pl.BlockSpec(memory_space=pltpu.SMEM)


def tiled(array):
    return array.reshape(2, 8, -1, LANES).transpose(0, 2, 1, 3)


def body(series, index_series, assign):
    t = tables(2.0 / FFT / 256.0)
    t = {name: jnp.asarray(table) for name, table in t.items()}
    x = tiled(series)
    y = tiled(index_series)
    halo = lax.ppermute(x[:, ROWS:], "ta", [(i, i + 1) for i in range(7)])
    params = pltpu.CompilerParams(vmem_limit_bytes=40 * 1024 * 1024)
    pre, x0, y0 = pl.pallas_call(
        local_kernel,
        out_shape=(
            jax.ShapeDtypeStruct((16, 2, ROWS, 2 * LANES), F32),
            jax.ShapeDtypeStruct((16, ROWS, 2 * LANES), F32),
            jax.ShapeDtypeStruct((16, ROWS, 2 * LANES), F32),
        ),
        in_specs=[SMEM] + [VMEM] * 6,
        out_specs=(VMEM,) * 3,
        scratch_shapes=[pltpu.VMEM((16 * 64, 2 * LANES), F32)],
        compiler_params=params,
        cost_estimate=pl.CostEstimate(flops=3_000_000_000, bytes_accessed=3_000_000, transcendentals=0),
        name="local_terms",
    )(assign, x.reshape(1024, LANES), y.reshape(1024, LANES), t["w1"], t["tw"], t["sign"], t["fwd"])
    out = pl.pallas_call(
        halo_kernel,
        out_shape=jax.ShapeDtypeStruct((1024, LANES), F32),
        in_specs=[VMEM] * 10,
        out_specs=VMEM,
        compiler_params=params,
        cost_estimate=pl.CostEstimate(flops=2_000_000_000, bytes_accessed=3_000_000, transcendentals=0),
        name="halo_and_lags",
    )(halo.reshape(512, LANES), pre, x0, y0, t["w1"], t["tw_halo"], t["tw"], t["fwd"], t["inv"], t["w4"])
    shares = lax.all_to_all(out.reshape(8, 128, LANES), "ta", 0, 0, tiled=True)
    total = jnp.sum(shares, axis=0).reshape(2, 2, 4, 8, LANES)
    both = total.transpose(0, 1, 3, 2, 4).reshape(2, 16, 512)
    return both[0], both[1]


def solution(mesh):
    return jax.shard_map(
        body,
        mesh=mesh,
        in_specs=(P("sa", "ta"), P(None, "ta"), P()),
        out_specs=(P("sa", "ta"), P("sa", "ta")),
        check_vma=False,
    )
```

```python
import functools
import math

import jax
import jax.numpy as jnp
import numpy as np
from jax import lax
from jax.experimental import pallas as pl
from jax.experimental.pallas import tpu as pltpu
from jax.sharding import PartitionSpec as P

LANES = 128
ROWS = 32
BLOCK = ROWS * LANES
FFT = 2 * BLOCK
BF16 = jnp.bfloat16
F32 = jnp.float32
W1 = 1024
W4 = W1 + 64
EARLY = 8
TW = W4 + ROWS


def twiddle(wide, i):
    return sum(
        wide[TW + (p * 3 + i // 2) * ROWS : TW + (p * 3 + i // 2 + 1) * ROWS, i % 2 * LANES : (i % 2 + 1) * LANES].astype(F32)
        for p in (2, 1, 0)
    )


def split_np(table):
    hi = table.astype(np.float32).astype(BF16)
    lo = (table - hi.astype(np.float64)).astype(np.float32).astype(BF16)
    return hi, lo


def tables():
    k1 = np.arange(ROWS)[:, None] + 0.5
    t1 = np.arange(ROWS)[None, :]
    first = 2.0 * math.pi * k1 * t1 / (2 * ROWS)
    w1 = np.concatenate([np.cos(first), -np.sin(first)], axis=0)
    w1_hi, w1_lo = split_np(w1)
    w1 = np.concatenate([w1_hi, w1_lo, w1_hi], axis=1)
    t2 = np.arange(LANES)[None, :]
    turn = 2.0 * math.pi * k1 * t2 / FFT
    sign = np.where(np.arange(ROWS) % 2 == 0, 1.0, -1.0)[:, None] * np.ones((1, LANES))
    twiddles = np.stack([np.cos(turn), np.sin(turn), np.sin(turn) * sign, -np.cos(turn) * sign, sign])
    second = 2.0 * math.pi * np.arange(LANES)[:, None] * np.arange(LANES)[None, :] / LANES
    c, s = np.cos(second), np.sin(second)
    fwd = np.concatenate([np.concatenate([c, -s], 1), np.concatenate([s, c], 1)], 0)
    inv = np.concatenate([np.concatenate([c, s], 1), np.concatenate([-s, c], 1)], 0)
    n1 = np.arange(ROWS).reshape(8, 4).T.reshape(-1)[:, None]
    last = 2.0 * math.pi * (np.arange(ROWS)[None, :] + 0.5) * n1 / (2 * ROWS)
    w4 = np.concatenate([np.cos(last), -np.sin(last)], axis=1) * (2.0 / FFT / 256.0)
    w4_hi, w4_lo = split_np(w4)
    w4 = np.concatenate([w4_hi, w4_lo, w4_hi], axis=1)
    wide = np.zeros((TW + 9 * ROWS, 2 * LANES), BF16)
    wide[:512] = np.concatenate(split_np(fwd))
    wide[512:1024] = np.concatenate(split_np(inv))
    wide[W1 : W1 + 64, :96] = w1
    wide[W4 : W4 + ROWS, :192] = w4
    rest = twiddles.astype(np.float32)
    for piece in range(3):
        part = rest.astype(BF16)
        rest = rest - part.astype(np.float32)
        for i in range(5):
            at = TW + (piece * 3 + i // 2) * ROWS
            wide[at : at + ROWS, i % 2 * LANES : (i % 2 + 1) * LANES] = part[i]
    return wide


def split(value):
    hi = value.astype(BF16)
    return hi, (value - hi.astype(F32)).astype(BF16)


def dot(a, b):
    return jnp.dot(a, b, preferred_element_type=F32)


def first_stage(blocks, w1, tw_c, tw_s):
    hi, lo = split(jnp.concatenate(blocks, axis=1))
    both = dot(w1, jnp.concatenate([hi, hi, lo], axis=0))
    done = []
    for i in range(2):
        re = both[:ROWS, i * LANES : (i + 1) * LANES]
        im = both[ROWS:, i * LANES : (i + 1) * LANES]
        done.append(jnp.concatenate([re * tw_c + im * tw_s, im * tw_c - re * tw_s], axis=1))
    return done


def second_stage(value, f_hi, f_lo):
    hi, lo = split(value)
    return dot(hi, f_hi) + dot(lo, f_hi) + dot(hi, f_lo)


def parts(value):
    return value[:, :LANES], value[:, LANES:]


def mul_conj(a, b):
    (ar, ai), (br, bi) = a, b
    return ar * br + ai * bi, ai * br - ar * bi


def forward(ref, starts, w1, tw_c, tw_s, f_hi, f_lo):
    staged = []
    for i in range(0, len(starts), 2):
        blocks = [ref[pl.ds(start, ROWS, stride=8), :] for start in starts[i : i + 2]]
        staged += first_stage(blocks, w1, tw_c, tw_s)
    return second_stage(jnp.concatenate(staged, axis=0), f_hi, f_lo)


def tails(source, step, series, target):
    for i, s in enumerate(series):
        target[pl.ds(i * ROWS, ROWS), :] = source[pl.ds(step * (s // 8) + step - 256 + s % 8, ROWS, stride=8), :]


def early_kernel(x_ref, out_ref):
    tails(x_ref, 512, range(EARLY), out_ref)


def late_kernel(x_ref, early_ref, out_ref):
    tails(x_ref, 512, range(EARLY, 16), out_ref)


def block_start(s, b):
    return (s // 8) * 512 + s % 8 + b * 256


def local_kernel(assign_ref, x_ref, y_ref, wide, pre_ref, x0_ref, y0_ref, ys_ref):
    base = lax.axis_index("sa") * 16
    w1 = wide[W1 : W1 + 64, :96]
    tw_c, tw_s, sign = (twiddle(wide, i) for i in (0, 1, 4))
    f_hi, f_lo = wide[:256], wide[256:512]
    group = 4

    def spectra(ref, g):
        starts = [block_start(s, b) for s in range(g, g + group) for b in range(2)]
        return forward(ref, starts, w1, tw_c, tw_s, f_hi, f_lo)

    for g in range(0, 16, group):
        ys_ref[pl.ds(g * 64, group * 64), :] = spectra(y_ref, g)
    for g in range(0, 16, group):
        spec = spectra(x_ref, g)
        for i in range(group):
            s = g + i
            x0 = spec[i * 64 : i * 64 + ROWS]
            x1 = parts(spec[i * 64 + ROWS : i * 64 + 64])
            x0_ref[s] = x0
            x0 = parts(x0)
            at = pl.multiple_of(assign_ref[base + s] * 64, 64)
            y0 = ys_ref[pl.ds(at, ROWS), :]
            y1 = parts(ys_ref[pl.ds(at + ROWS, ROWS), :])
            y0_ref[s] = y0
            y0 = parts(y0)
            window = (x1[0] - sign * x0[1], x1[1] + sign * x0[0])
            re, im = mul_conj(x1, window)
            pre_ref[s, 0] = jnp.concatenate([re + x0[0] * x0[0] + x0[1] * x0[1], im], axis=1)
            re, im = mul_conj(y1, window)
            re0, im0 = mul_conj(y0, x0)
            pre_ref[s, 1] = jnp.concatenate([re + re0, im + im0], axis=1)


def halo_kernel(series, h_ref, pre_ref, x0_ref, y0_ref, wide, *refs):
    out_ref = refs[-1]
    w1 = wide[W1 : W1 + 64, :96]
    w4 = wide[W4 : W4 + ROWS, :192]
    tw_c, tw_s, twh_c, twh_s = (twiddle(wide, i) for i in range(4))
    has_halo = jnp.where(lax.axis_index("ta") == 0, 0.0, 1.0)
    f_hi, f_lo = wide[:256], wide[256:512]
    i_hi, i_lo = wide[512:768], wide[768:1024]
    size = min(len(series), 8)
    for g in range(0, len(series), size):
        staged = []
        for i in range(g, g + size, 2):
            blocks = [h_ref[pl.ds(b * ROWS, ROWS), :] for b in (i, i + 1)]
            staged += first_stage(blocks, w1, twh_c * has_halo, twh_s * has_halo)
        spec = second_stage(jnp.concatenate(staged, axis=0), f_hi, f_lo)
        whole = []
        for i, s in enumerate(series[g : g + size]):
            before = parts(spec[i * ROWS : (i + 1) * ROWS])
            for c, other in enumerate((x0_ref, y0_ref)):
                re, im = mul_conj(parts(other[s]), before)
                whole.append(pre_ref[s, c] + jnp.concatenate([re, im], axis=1))
        back = second_stage(jnp.concatenate(whole, axis=0), i_hi, i_lo)
        for i, s in enumerate(series[g : g + size]):
            turned = []
            for c in range(2):
                re, im = parts(back[(2 * i + c) * ROWS : (2 * i + c + 1) * ROWS])
                turned.append(jnp.concatenate([re * tw_c - im * tw_s, re * tw_s + im * tw_c], axis=0))
            hi, lo = split(jnp.concatenate(turned, axis=1))
            lags = dot(w4, jnp.concatenate([hi, hi, lo], axis=0))
            for c in range(2):
                for low in range(4):
                    out_ref[pl.ds(c * 64 + s // 8 * 32 + low * 8 + s % 8, 8, stride=128), :] = lags[
                        low * 8 : low * 8 + 8, c * LANES : (c + 1) * LANES
                    ]


VMEM = pl.BlockSpec(memory_space=pltpu.VMEM)
SMEM = pl.BlockSpec(memory_space=pltpu.SMEM)
ANY = pl.BlockSpec(memory_space=pl.ANY)
RING = [(i, (i + 1) % 8) for i in range(8)]


def flat(array):
    return array.reshape(2, 8, -1, LANES).transpose(0, 2, 1, 3).reshape(-1, LANES)


def floats(*shape):
    return jax.ShapeDtypeStruct(shape, F32)


def cost(flops, nbytes):
    return pl.CostEstimate(flops=flops, bytes_accessed=nbytes, transcendentals=0)


def body(series, index_series, assign):
    wide = tables()
    params = pltpu.CompilerParams(vmem_limit_bytes=40 * 1024 * 1024)
    x, y = flat(series), flat(index_series)
    early = pl.pallas_call(
        early_kernel,
        out_shape=floats(EARLY * ROWS, LANES),
        in_specs=[VMEM],
        out_specs=VMEM,
        compiler_params=params,
        cost_estimate=cost(0, 262_144),
        name="early_tails",
    )(x)
    late = pl.pallas_call(
        late_kernel,
        out_shape=floats((16 - EARLY) * ROWS, LANES),
        in_specs=[VMEM, ANY],
        out_specs=VMEM,
        compiler_params=params,
        cost_estimate=cost(1_000_000_000, 2_000_000),
        name="late_tails",
    )(x, early)
    halos = [lax.ppermute(tail, "ta", RING) for tail in (early, late)]
    wide = jnp.asarray(wide)
    spec = (16, ROWS, 2 * LANES)
    local = pl.pallas_call(
        local_kernel,
        out_shape=(floats(16, 2, ROWS, 2 * LANES), floats(*spec), floats(*spec)),
        in_specs=[SMEM] + [VMEM] * 3,
        out_specs=(VMEM,) * 3,
        scratch_shapes=[pltpu.VMEM((1024, 2 * LANES), F32)],
        compiler_params=params,
        cost_estimate=cost(3_000_000_000, 3_000_000),
        name="local_terms",
    )(assign, x, y, wide)

    def lags(series, *operands):
        return pl.pallas_call(
            functools.partial(halo_kernel, series),
            out_shape=floats(1024, LANES),
            in_specs=[VMEM] * len(operands),
            out_specs=VMEM,
            input_output_aliases={5: 0} if len(operands) > 5 else {},
            compiler_params=params,
            cost_estimate=cost(1_000_000_000, 2_000_000),
            name="halo_and_lags",
        )(*operands)

    out = lags(range(EARLY), halos[0], *local, wide)
    out = lags(range(EARLY, 16), halos[1], *local, wide, out)
    shares = lax.all_to_all(out.reshape(8, 128, LANES), "ta", 0, 0, tiled=True)
    total = jnp.sum(shares, axis=0).reshape(2, 2, 4, 8, LANES)
    both = total.transpose(0, 1, 3, 2, 4).reshape(2, 16, 512)
    return both[0], both[1]


def solution(mesh):
    return jax.shard_map(
        body,
        mesh=mesh,
        in_specs=(P("sa", "ta"), P(None, "ta"), P()),
        out_specs=(P("sa", "ta"), P("sa", "ta")),
        check_vma=False,
    )
```

```python
import functools
import math

import jax
import jax.numpy as jnp
import numpy as np
from jax import lax
from jax.experimental import pallas as pl
from jax.experimental.pallas import tpu as pltpu
from jax.sharding import PartitionSpec as P

LANES = 128
ROWS = 32
BLOCK = ROWS * LANES
FFT = 2 * BLOCK
BF16 = jnp.bfloat16
F32 = jnp.float32
W1 = 1024
W4 = W1 + 64
SPLITS = (0, 6, 12, 16)
TW = W4 + ROWS


def twiddle(wide, i):
    return sum(
        wide[TW + (p * 3 + i // 2) * ROWS : TW + (p * 3 + i // 2 + 1) * ROWS, i % 2 * LANES : (i % 2 + 1) * LANES].astype(F32)
        for p in (2, 1, 0)
    )


def split_np(table):
    hi = table.astype(np.float32).astype(BF16)
    lo = (table - hi.astype(np.float64)).astype(np.float32).astype(BF16)
    return hi, lo


def tables():
    k1 = np.arange(ROWS)[:, None] + 0.5
    t1 = np.arange(ROWS)[None, :]
    first = 2.0 * math.pi * k1 * t1 / (2 * ROWS)
    w1 = np.concatenate([np.cos(first), -np.sin(first)], axis=0)
    w1_hi, w1_lo = split_np(w1)
    w1 = np.concatenate([w1_hi, w1_lo, w1_hi], axis=1)
    t2 = np.arange(LANES)[None, :]
    turn = 2.0 * math.pi * k1 * t2 / FFT
    sign = np.where(np.arange(ROWS) % 2 == 0, 1.0, -1.0)[:, None] * np.ones((1, LANES))
    twiddles = np.stack([np.cos(turn), np.sin(turn), np.sin(turn) * sign, -np.cos(turn) * sign, sign])
    second = 2.0 * math.pi * np.arange(LANES)[:, None] * np.arange(LANES)[None, :] / LANES
    c, s = np.cos(second), np.sin(second)
    fwd = np.concatenate([np.concatenate([c, -s], 1), np.concatenate([s, c], 1)], 0)
    inv = np.concatenate([np.concatenate([c, s], 1), np.concatenate([-s, c], 1)], 0)
    n1 = np.arange(ROWS).reshape(8, 4).T.reshape(-1)[:, None]
    last = 2.0 * math.pi * (np.arange(ROWS)[None, :] + 0.5) * n1 / (2 * ROWS)
    w4 = np.concatenate([np.cos(last), -np.sin(last)], axis=1) * (2.0 / FFT / 256.0)
    w4_hi, w4_lo = split_np(w4)
    w4 = np.concatenate([w4_hi, w4_lo, w4_hi], axis=1)
    wide = np.zeros((TW + 9 * ROWS, 2 * LANES), BF16)
    wide[:512] = np.concatenate(split_np(fwd))
    wide[512:1024] = np.concatenate(split_np(inv))
    wide[W1 : W1 + 64, :96] = w1
    wide[W4 : W4 + ROWS, :192] = w4
    rest = twiddles.astype(np.float32)
    for piece in range(3):
        part = rest.astype(BF16)
        rest = rest - part.astype(np.float32)
        for i in range(5):
            at = TW + (piece * 3 + i // 2) * ROWS
            wide[at : at + ROWS, i % 2 * LANES : (i % 2 + 1) * LANES] = part[i]
    return wide


def split(value):
    hi = value.astype(BF16)
    return hi, (value - hi.astype(F32)).astype(BF16)


def dot(a, b):
    return jnp.dot(a, b, preferred_element_type=F32)


def first_stage(blocks, w1, tw_c, tw_s):
    hi, lo = split(jnp.concatenate(blocks, axis=1))
    both = dot(w1, jnp.concatenate([hi, hi, lo], axis=0))
    done = []
    for i in range(2):
        re = both[:ROWS, i * LANES : (i + 1) * LANES]
        im = both[ROWS:, i * LANES : (i + 1) * LANES]
        done.append(jnp.concatenate([re * tw_c + im * tw_s, im * tw_c - re * tw_s], axis=1))
    return done


def second_stage(value, f_hi, f_lo):
    hi, lo = split(value)
    return dot(jnp.concatenate([hi, lo, hi], axis=1), jnp.concatenate([f_hi, f_hi, f_lo], axis=0))


def parts(value):
    return value[:, :LANES], value[:, LANES:]


def mul_conj(a, b):
    (ar, ai), (br, bi) = a, b
    return ar * br + ai * bi, ai * br - ar * bi


def forward(ref, starts, w1, tw_c, tw_s, f_hi, f_lo):
    staged = []
    for i in range(0, len(starts), 2):
        blocks = [ref[pl.ds(start, ROWS, stride=8), :] for start in starts[i : i + 2]]
        staged += first_stage(blocks, w1, tw_c, tw_s)
    return second_stage(jnp.concatenate(staged, axis=0), f_hi, f_lo)


def tails(source, step, series, target):
    for i, s in enumerate(series):
        target[pl.ds(i * ROWS, ROWS), :] = source[pl.ds(step * (s // 8) + step - 256 + s % 8, ROWS, stride=8), :]


def tails_kernel(series, x_ref, *refs):
    tails(x_ref, 512, series, refs[-1])


def block_start(s, b):
    return (s // 8) * 512 + s % 8 + b * 256


def local_kernel(assign_ref, x_ref, y_ref, wide, pre_ref, x0_ref, y0_ref, ys_ref):
    base = lax.axis_index("sa") * 16
    w1 = wide[W1 : W1 + 64, :96]
    tw_c, tw_s, sign = (twiddle(wide, i) for i in (0, 1, 4))
    f_hi, f_lo = wide[:256], wide[256:512]
    group = 4

    def spectra(ref, g):
        starts = [block_start(s, b) for s in range(g, g + group) for b in range(2)]
        return forward(ref, starts, w1, tw_c, tw_s, f_hi, f_lo)

    for g in range(0, 16, group):
        ys_ref[pl.ds(g * 64, group * 64), :] = spectra(y_ref, g)
    for g in range(0, 16, group):
        spec = spectra(x_ref, g)
        for i in range(group):
            s = g + i
            x0 = spec[i * 64 : i * 64 + ROWS]
            x1 = parts(spec[i * 64 + ROWS : i * 64 + 64])
            x0_ref[s] = x0
            x0 = parts(x0)
            at = pl.multiple_of(assign_ref[base + s] * 64, 64)
            y0 = ys_ref[pl.ds(at, ROWS), :]
            y1 = parts(ys_ref[pl.ds(at + ROWS, ROWS), :])
            y0_ref[s] = y0
            y0 = parts(y0)
            window = (x1[0] - sign * x0[1], x1[1] + sign * x0[0])
            re, im = mul_conj(x1, window)
            pre_ref[s, 0] = jnp.concatenate([re + x0[0] * x0[0] + x0[1] * x0[1], im], axis=1)
            re, im = mul_conj(y1, window)
            re0, im0 = mul_conj(y0, x0)
            pre_ref[s, 1] = jnp.concatenate([re + re0, im + im0], axis=1)


def halo_kernel(series, h_ref, pre_ref, x0_ref, y0_ref, wide, *refs):
    out_ref = refs[-1]
    w1 = wide[W1 : W1 + 64, :96]
    w4 = wide[W4 : W4 + ROWS, :192]
    tw_c, tw_s, twh_c, twh_s = (twiddle(wide, i) for i in range(4))
    has_halo = jnp.where(lax.axis_index("ta") == 0, 0.0, 1.0)
    f_hi, f_lo = wide[:256], wide[256:512]
    i_hi, i_lo = wide[512:768], wide[768:1024]
    size = min(len(series), 8)
    for g in range(0, len(series), size):
        staged = []
        for i in range(g, g + size, 2):
            blocks = [h_ref[pl.ds(b * ROWS, ROWS), :] for b in (i, i + 1)]
            staged += first_stage(blocks, w1, twh_c * has_halo, twh_s * has_halo)
        spec = second_stage(jnp.concatenate(staged, axis=0), f_hi, f_lo)
        whole = []
        for i, s in enumerate(series[g : g + size]):
            before = parts(spec[i * ROWS : (i + 1) * ROWS])
            for c, other in enumerate((x0_ref, y0_ref)):
                re, im = mul_conj(parts(other[s]), before)
                whole.append(pre_ref[s, c] + jnp.concatenate([re, im], axis=1))
        back = second_stage(jnp.concatenate(whole, axis=0), i_hi, i_lo)
        for i, s in enumerate(series[g : g + size]):
            turned = []
            for c in range(2):
                re, im = parts(back[(2 * i + c) * ROWS : (2 * i + c + 1) * ROWS])
                turned.append(jnp.concatenate([re * tw_c - im * tw_s, re * tw_s + im * tw_c], axis=0))
            hi, lo = split(jnp.concatenate(turned, axis=1))
            lags = dot(w4, jnp.concatenate([hi, hi, lo], axis=0))
            for c in range(2):
                for low in range(4):
                    out_ref[pl.ds(c * 64 + s // 8 * 32 + low * 8 + s % 8, 8, stride=128), :] = lags[
                        low * 8 : low * 8 + 8, c * LANES : (c + 1) * LANES
                    ]


VMEM = pl.BlockSpec(memory_space=pltpu.VMEM)
SMEM = pl.BlockSpec(memory_space=pltpu.SMEM)
ANY = pl.BlockSpec(memory_space=pl.ANY)
RING = [(i, (i + 1) % 8) for i in range(8)]


def flat(array):
    return array.reshape(2, 8, -1, LANES).transpose(0, 2, 1, 3).reshape(-1, LANES)


def floats(*shape):
    return jax.ShapeDtypeStruct(shape, F32)


def cost(flops, nbytes):
    return pl.CostEstimate(flops=flops, bytes_accessed=nbytes, transcendentals=0)


def body(series, index_series, assign):
    wide = tables()
    params = pltpu.CompilerParams(vmem_limit_bytes=40 * 1024 * 1024)
    x, y = flat(series), flat(index_series)
    pieces = [range(*ends) for ends in zip(SPLITS, SPLITS[1:])]
    sent = []
    for series in pieces:
        sent.append(
            pl.pallas_call(
                functools.partial(tails_kernel, series),
                out_shape=floats(len(series) * ROWS, LANES),
                in_specs=[VMEM] + [ANY] * len(sent[-1:]),
                out_specs=VMEM,
                compiler_params=params,
                cost_estimate=cost(1_000_000_000, 2_000_000),
                name="tails",
            )(x, *sent[-1:])
        )
    halos = [lax.ppermute(tail, "ta", RING) for tail in sent]
    wide = jnp.asarray(wide)
    spec = (16, ROWS, 2 * LANES)
    local = pl.pallas_call(
        local_kernel,
        out_shape=(floats(16, 2, ROWS, 2 * LANES), floats(*spec), floats(*spec)),
        in_specs=[SMEM] + [VMEM] * 3,
        out_specs=(VMEM,) * 3,
        scratch_shapes=[pltpu.VMEM((1024, 2 * LANES), F32)],
        compiler_params=params,
        cost_estimate=cost(3_000_000_000, 3_000_000),
        name="local_terms",
    )(assign, x, y, wide)

    def lags(series, *operands):
        return pl.pallas_call(
            functools.partial(halo_kernel, series),
            out_shape=floats(1024, LANES),
            in_specs=[VMEM] * len(operands),
            out_specs=VMEM,
            input_output_aliases={5: 0} if len(operands) > 5 else {},
            compiler_params=params,
            cost_estimate=cost(1_000_000_000, 2_000_000),
            name="halo_and_lags",
        )(*operands)

    out = ()
    for series, halo in zip(pieces, halos):
        out = (lags(series, halo, *local, wide, *out),)
    (out,) = out
    shares = lax.all_to_all(out.reshape(8, 128, LANES), "ta", 0, 0, tiled=True)
    total = jnp.sum(shares, axis=0).reshape(2, 2, 4, 8, LANES)
    both = total.transpose(0, 1, 3, 2, 4).reshape(2, 16, 512)
    return both[0], both[1]


def solution(mesh):
    return jax.shard_map(
        body,
        mesh=mesh,
        in_specs=(P("sa", "ta"), P(None, "ta"), P()),
        out_specs=(P("sa", "ta"), P("sa", "ta")),
        check_vma=False,
    )
```

```python
import functools
import math

import jax
import jax.numpy as jnp
import numpy as np
from jax import lax
from jax.experimental import pallas as pl
from jax.experimental.pallas import tpu as pltpu
from jax.sharding import PartitionSpec as P

LANES = 128
ROWS = 32
BLOCK = ROWS * LANES
FFT = 2 * BLOCK
BF16 = jnp.bfloat16
F32 = jnp.float32
W1 = 1024
W4 = W1 + 64
SPLITS = (0, 4, 12, 16)
TW = W4 + ROWS


def twiddle(wide, i):
    return sum(
        wide[TW + (p * 3 + i // 2) * ROWS : TW + (p * 3 + i // 2 + 1) * ROWS, i % 2 * LANES : (i % 2 + 1) * LANES].astype(F32)
        for p in (2, 1, 0)
    )


def split_np(table):
    hi = table.astype(np.float32).astype(BF16)
    lo = (table - hi.astype(np.float64)).astype(np.float32).astype(BF16)
    return hi, lo


def tables():
    k1 = np.arange(ROWS)[:, None] + 0.5
    t1 = np.arange(ROWS)[None, :]
    first = 2.0 * math.pi * k1 * t1 / (2 * ROWS)
    w1 = np.concatenate([np.cos(first), -np.sin(first)], axis=0)
    w1_hi, w1_lo = split_np(w1)
    w1 = np.concatenate([w1_hi, w1_lo, w1_hi], axis=1)
    t2 = np.arange(LANES)[None, :]
    turn = 2.0 * math.pi * k1 * t2 / FFT
    sign = np.where(np.arange(ROWS) % 2 == 0, 1.0, -1.0)[:, None] * np.ones((1, LANES))
    twiddles = np.stack([np.cos(turn), np.sin(turn), np.sin(turn) * sign, -np.cos(turn) * sign, sign])
    second = 2.0 * math.pi * np.arange(LANES)[:, None] * np.arange(LANES)[None, :] / LANES
    c, s = np.cos(second), np.sin(second)
    fwd = np.concatenate([np.concatenate([c, -s], 1), np.concatenate([s, c], 1)], 0)
    inv = np.concatenate([np.concatenate([c, s], 1), np.concatenate([-s, c], 1)], 0)
    n1 = np.arange(ROWS).reshape(8, 4).T.reshape(-1)[:, None]
    last = 2.0 * math.pi * (np.arange(ROWS)[None, :] + 0.5) * n1 / (2 * ROWS)
    w4 = np.concatenate([np.cos(last), -np.sin(last)], axis=1) * (2.0 / FFT / 256.0)
    w4_hi, w4_lo = split_np(w4)
    w4 = np.concatenate([w4_hi, w4_lo, w4_hi], axis=1)
    wide = np.zeros((TW + 9 * ROWS, 2 * LANES), BF16)
    wide[:512] = np.concatenate(split_np(fwd))
    wide[512:1024] = np.concatenate(split_np(inv))
    wide[W1 : W1 + 64, :96] = w1
    wide[W4 : W4 + ROWS, :192] = w4
    rest = twiddles.astype(np.float32)
    for piece in range(3):
        part = rest.astype(BF16)
        rest = rest - part.astype(np.float32)
        for i in range(5):
            at = TW + (piece * 3 + i // 2) * ROWS
            wide[at : at + ROWS, i % 2 * LANES : (i % 2 + 1) * LANES] = part[i]
    return wide


def split(value):
    hi = value.astype(BF16)
    return hi, (value - hi.astype(F32)).astype(BF16)


def dot(a, b):
    return jnp.dot(a, b, preferred_element_type=F32)


def first_stage(blocks, w1, tw_c, tw_s):
    hi, lo = split(jnp.concatenate(blocks, axis=1))
    both = dot(w1, jnp.concatenate([hi, hi, lo], axis=0))
    done = []
    for i in range(2):
        re = both[:ROWS, i * LANES : (i + 1) * LANES]
        im = both[ROWS:, i * LANES : (i + 1) * LANES]
        done.append(jnp.concatenate([re * tw_c + im * tw_s, im * tw_c - re * tw_s], axis=1))
    return done


def second_stage(value, f_hi, f_lo):
    hi, lo = split(value)
    return dot(jnp.concatenate([hi, lo, hi], axis=1), jnp.concatenate([f_hi, f_hi, f_lo], axis=0))


def parts(value):
    return value[:, :LANES], value[:, LANES:]


def mul_conj(a, b):
    (ar, ai), (br, bi) = a, b
    return ar * br + ai * bi, ai * br - ar * bi


def forward(ref, starts, w1, tw_c, tw_s, f_hi, f_lo):
    staged = []
    for i in range(0, len(starts), 2):
        blocks = [ref[pl.ds(start, ROWS, stride=8), :] for start in starts[i : i + 2]]
        staged += first_stage(blocks, w1, tw_c, tw_s)
    return second_stage(jnp.concatenate(staged, axis=0), f_hi, f_lo)


def tails(source, step, series, target):
    for i, s in enumerate(series):
        target[pl.ds(i * ROWS, ROWS), :] = source[pl.ds(step * (s // 8) + step - 256 + s % 8, ROWS, stride=8), :]


def tails_kernel(series, x_ref, *refs):
    tails(x_ref, 512, series, refs[-1])


def block_start(s, b):
    return (s // 8) * 512 + s % 8 + b * 256


def local_kernel(assign_ref, x_ref, y_ref, wide, pre_ref, x0_ref, y0_ref, ys_ref):
    base = lax.axis_index("sa") * 16
    w1 = wide[W1 : W1 + 64, :96]
    tw_c, tw_s, sign = (twiddle(wide, i) for i in (0, 1, 4))
    f_hi, f_lo = wide[:256], wide[256:512]
    group = 4

    def spectra(ref, g):
        starts = [block_start(s, b) for s in range(g, g + group) for b in range(2)]
        return forward(ref, starts, w1, tw_c, tw_s, f_hi, f_lo)

    for g in range(0, 16, group):
        ys_ref[pl.ds(g * 64, group * 64), :] = spectra(y_ref, g)
    for g in range(0, 16, group):
        spec = spectra(x_ref, g)
        for i in range(group):
            s = g + i
            x0 = spec[i * 64 : i * 64 + ROWS]
            x1 = parts(spec[i * 64 + ROWS : i * 64 + 64])
            x0_ref[s] = x0
            x0 = parts(x0)
            at = pl.multiple_of(assign_ref[base + s] * 64, 64)
            y0 = ys_ref[pl.ds(at, ROWS), :]
            y1 = parts(ys_ref[pl.ds(at + ROWS, ROWS), :])
            y0_ref[s] = y0
            y0 = parts(y0)
            window = (x1[0] - sign * x0[1], x1[1] + sign * x0[0])
            re, im = mul_conj(x1, window)
            pre_ref[s, 0] = jnp.concatenate([re + x0[0] * x0[0] + x0[1] * x0[1], im], axis=1)
            re, im = mul_conj(y1, window)
            re0, im0 = mul_conj(y0, x0)
            pre_ref[s, 1] = jnp.concatenate([re + re0, im + im0], axis=1)


def halo_kernel(series, h_ref, pre_ref, x0_ref, y0_ref, wide, *refs):
    out_ref = refs[-1]
    w1 = wide[W1 : W1 + 64, :96]
    w4 = wide[W4 : W4 + ROWS, :192]
    tw_c, tw_s, twh_c, twh_s = (twiddle(wide, i) for i in range(4))
    has_halo = jnp.where(lax.axis_index("ta") == 0, 0.0, 1.0)
    f_hi, f_lo = wide[:256], wide[256:512]
    i_hi, i_lo = wide[512:768], wide[768:1024]
    size = min(len(series), 8)
    for g in range(0, len(series), size):
        staged = []
        for i in range(g, g + size, 2):
            blocks = [h_ref[pl.ds(b * ROWS, ROWS), :] for b in (i, i + 1)]
            staged += first_stage(blocks, w1, twh_c * has_halo, twh_s * has_halo)
        spec = second_stage(jnp.concatenate(staged, axis=0), f_hi, f_lo)
        whole = []
        for i, s in enumerate(series[g : g + size]):
            before = parts(spec[i * ROWS : (i + 1) * ROWS])
            for c, other in enumerate((x0_ref, y0_ref)):
                re, im = mul_conj(parts(other[s]), before)
                whole.append(pre_ref[s, c] + jnp.concatenate([re, im], axis=1))
        back = second_stage(jnp.concatenate(whole, axis=0), i_hi, i_lo)
        for i, s in enumerate(series[g : g + size]):
            turned = []
            for c in range(2):
                re, im = parts(back[(2 * i + c) * ROWS : (2 * i + c + 1) * ROWS])
                turned.append(jnp.concatenate([re * tw_c - im * tw_s, re * tw_s + im * tw_c], axis=0))
            hi, lo = split(jnp.concatenate(turned, axis=1))
            lags = dot(w4, jnp.concatenate([hi, hi, lo], axis=0))
            for c in range(2):
                for low in range(4):
                    out_ref[pl.ds(c * 64 + s // 8 * 32 + low * 8 + s % 8, 8, stride=128), :] = lags[
                        low * 8 : low * 8 + 8, c * LANES : (c + 1) * LANES
                    ]


def sum_kernel(shares_ref, auto_ref, cross_ref):
    for c, ref in enumerate((auto_ref, cross_ref)):
        ref[...] = sum(shares_ref[i, pl.ds(c * 64, 64), :] for i in range(8))


VMEM = pl.BlockSpec(memory_space=pltpu.VMEM)
SMEM = pl.BlockSpec(memory_space=pltpu.SMEM)
ANY = pl.BlockSpec(memory_space=pl.ANY)
RING = [(i, (i + 1) % 8) for i in range(8)]


def flat(array):
    return array.reshape(2, 8, -1, LANES).transpose(0, 2, 1, 3).reshape(-1, LANES)


def floats(*shape):
    return jax.ShapeDtypeStruct(shape, F32)


def cost(flops, nbytes):
    return pl.CostEstimate(flops=flops, bytes_accessed=nbytes, transcendentals=0)


def body(series, index_series, assign):
    wide = tables()
    params = pltpu.CompilerParams(vmem_limit_bytes=40 * 1024 * 1024)
    x, y = flat(series), flat(index_series)
    pieces = [range(*ends) for ends in zip(SPLITS, SPLITS[1:])]
    sent = []
    for series in pieces:
        sent.append(
            pl.pallas_call(
                functools.partial(tails_kernel, series),
                out_shape=floats(len(series) * ROWS, LANES),
                in_specs=[VMEM] + [ANY] * len(sent[-1:]),
                out_specs=VMEM,
                compiler_params=params,
                cost_estimate=cost(1_000_000_000, 2_000_000),
                name="tails",
            )(x, *sent[-1:])
        )
    halos = [lax.ppermute(tail, "ta", RING) for tail in sent]
    wide = jnp.asarray(wide)
    spec = (16, ROWS, 2 * LANES)
    local = pl.pallas_call(
        local_kernel,
        out_shape=(floats(16, 2, ROWS, 2 * LANES), floats(*spec), floats(*spec)),
        in_specs=[SMEM] + [VMEM] * 3,
        out_specs=(VMEM,) * 3,
        scratch_shapes=[pltpu.VMEM((1024, 2 * LANES), F32)],
        compiler_params=params,
        cost_estimate=cost(3_000_000_000, 3_000_000),
        name="local_terms",
    )(assign, x, y, wide)

    def lags(series, *operands):
        return pl.pallas_call(
            functools.partial(halo_kernel, series),
            out_shape=floats(1024, LANES),
            in_specs=[VMEM] * len(operands),
            out_specs=VMEM,
            input_output_aliases={5: 0} if len(operands) > 5 else {},
            compiler_params=params,
            cost_estimate=cost(1_000_000_000, 2_000_000),
            name="halo_and_lags",
        )(*operands)

    out = ()
    for series, halo in zip(pieces, halos):
        out = (lags(series, halo, *local, wide, *out),)
    (out,) = out
    shares = lax.all_to_all(out.reshape(8, 128, LANES), "ta", 0, 0, tiled=True)
    sums = pl.pallas_call(
        sum_kernel,
        out_shape=(floats(64, LANES),) * 2,
        in_specs=[VMEM],
        out_specs=(VMEM,) * 2,
        compiler_params=params,
        cost_estimate=cost(0, 600_000),
        name="summed",
    )(shares)
    return tuple(s.reshape(2, 4, 8, LANES).transpose(0, 2, 1, 3).reshape(16, 512) for s in sums)


def solution(mesh):
    return jax.shard_map(
        body,
        mesh=mesh,
        in_specs=(P("sa", "ta"), P(None, "ta"), P()),
        out_specs=(P("sa", "ta"), P("sa", "ta")),
        check_vma=False,
    )
```
